512 devices in a mesh: dp: 8 (over y, core), node: 64 (over z, x).
Axes of the slice: x: 4, y: 4, z: 16, core: 2. Of those that a mesh axis runs over, the one named last changes fastest.
Arguments:
- leaf_logp: float32 [128, 32, 1024], P('node', None, 'dp'), may hold values from -108 to 0, as said below
- weights: bfloat16 [128, 32, 1024], P('node'), may hold values from 0.0099487305 to 1
- upper_flows: float32 [128, 32, 1024], P('node', None, 'dp'), may hold values from 0.01 to 1
- leaf_asks: int32 [64, 64], P('node'), may hold values from 0 to 1
- prod_asks: int32 [64, 64], P('node'), may hold values from 0 to 1
- prod_child: int32 [128, 8], P('node'), may hold values from 0 to 63
- prod_valid: int32 [128, 8], P('node'), may hold values 0 or 1
- sum_child: int32 [128, 32], P('node'), may hold values from 0 to 63
- sum_valid: int32 [128, 32], P('node'), may hold values from 0 to 1, as said below
Outputs:
- sum_loglik: float32 [128, 32, 1024], P('node', None, 'dp')
- weight_flows: float32 [128, 32, 1024], P('node', None, 'dp')
- prod_flows: float32 [128, 32, 1024], P('node', None, 'dp')
The draws below stay inside these ranges and needn't reach their ends.
Inputs may be any that keep to these rules, and one draw needn't show every extreme that they name: `leaf_logp`: log-probabilities, so no entry is positive. `leaf_asks`: entry (d, o) is which of owner o's 2 blocks device d reads. `prod_asks`: entry (d, o) is which of owner o's 2 blocks device d reads. `sum_valid`: the first child slot of every sum block is valid.
All inputs are finite; a program needn't handle non-finite values. No bound on the sum of `prod_valid` on one device may be relied on, other than what follows from the above.
Results may differ from the reference program's by a relative error of at most 0.0022.
Values sent between devices are 32-bit elements; how exact they have to be, the bound alone decides.
A program may use at most 64 MiB of HBM per device.

```python
import math
import jax
import jax.numpy as jnp
from jax import lax

K = 32
BLK_DEV = 2
PE = 8
SE = 32
OWNERS = 64
NBLK = 128
TOKENS = 1024


def draw_leaf_logp(key, part):
    first_key, second_key = jax.random.split(key)
    tok_scale = jnp.exp(jax.random.uniform(first_key, (1, 1, TOKENS), jnp.float32, jnp.log(2.0), jnp.log(25.0)))
    rough = jax.random.uniform(second_key, (NBLK, K, TOKENS), jnp.float32, 0.5, 1.5)
    return -(tok_scale * rough)


def draw_sum_valid(key, part):
    picks = jax.random.randint(key, (NBLK, SE), 0, 4)
    column = lax.broadcasted_iota(jnp.int32, (NBLK, SE), 1)
    return jnp.where((picks > 0) | (column == 0), 1, 0).astype(jnp.int32)


def plant(drawn, stream_key, smallest, top_value):
    longest = drawn.shape.index(max(drawn.shape))
    spots = []
    for shift in (0, 1):
        where = [jax.random.randint(jax.random.fold_in(stream_key, axis), (), 0, length) for axis, length in enumerate(drawn.shape)]
        where[longest] = (where[longest] + shift) % drawn.shape[longest]
        spots.append(tuple(where))
    return drawn.at[spots[0]].set(smallest).at[spots[1]].set(top_value)


def block_levels(own_key, shape, pieces, low, high):
    factor_of, own = 1.0, jax.random.fold_in(own_key, 6)
    for axis_at, shards_of in pieces:
        steps = jnp.exp(jax.random.uniform(jax.random.fold_in(own, axis_at), (shards_of,), jnp.float32, low / len(pieces), high / len(pieces)))
        factor_of = factor_of * jnp.repeat(steps, shape[axis_at] // shards_of).reshape([-1 if axis == axis_at else 1 for axis in range(len(shape))])
    return factor_of


def setup_inputs(seed: int = 0) -> dict:
    arg_keys = jax.random.split(jax.random.key(seed), 10)
    leaf_logp = draw_leaf_logp(jax.random.fold_in(arg_keys[9], 71), 0)
    weights = jnp.clip(jnp.exp(math.log(1.0) - 4.61031033 * jax.random.uniform(arg_keys[1], (NBLK, K, SE * K), jnp.float32) ** block_levels(arg_keys[1], (NBLK, K, SE * K), ((0, 64),), -0.2, 0.2)), 0.0099487305, 1.0).astype(jnp.bfloat16)
    upper_flows = jnp.clip(jnp.exp(math.log(1.0) - 4.6051702 * jax.random.uniform(arg_keys[2], (NBLK, K, TOKENS), jnp.float32) ** block_levels(arg_keys[2], (NBLK, K, TOKENS), ((0, 64), (2, 8)), -0.2, 0.2)), 0.01, 1.0)
    leaf_asks = plant(jax.random.randint(arg_keys[3], (OWNERS, OWNERS), 0, BLK_DEV), jax.random.fold_in(arg_keys[3], 1), 0, BLK_DEV - 1).astype(jnp.int32)
    prod_asks = plant(jax.random.randint(arg_keys[4], (OWNERS, OWNERS), 0, BLK_DEV), jax.random.fold_in(arg_keys[4], 1), 0, BLK_DEV - 1).astype(jnp.int32)
    prod_child = plant(jax.random.randint(arg_keys[5], (NBLK, PE), 0, OWNERS), jax.random.fold_in(arg_keys[5], 1), 0, OWNERS - 1).astype(jnp.int32)
    prod_valid = plant((jax.random.randint(arg_keys[6], (NBLK, PE), 0, 4) < 3).astype(jnp.int32), jax.random.fold_in(arg_keys[6], 1), 0, 1)
    sum_child = plant(jax.random.randint(arg_keys[7], (NBLK, SE), 0, OWNERS), jax.random.fold_in(arg_keys[7], 1), 0, OWNERS - 1).astype(jnp.int32)
    sum_valid = draw_sum_valid(jax.random.fold_in(arg_keys[9], 71), 0)
    return dict(leaf_logp=leaf_logp, weights=weights, upper_flows=upper_flows, leaf_asks=leaf_asks, prod_asks=prod_asks, prod_child=prod_child, prod_valid=prod_valid, sum_child=sum_child, sum_valid=sum_valid)


def reference(leaf_logp, weights, upper_flows, leaf_asks, prod_asks, prod_child, prod_valid, sum_child, sum_valid):
    owner_idx = (jnp.arange(NBLK) // BLK_DEV).astype(jnp.int32)
    leaf_ids = (prod_child * BLK_DEV + leaf_asks[owner_idx[:, None], prod_child]).astype(jnp.int32)
    sum_ids = (sum_child * BLK_DEV + prod_asks[owner_idx[:, None], sum_child]).astype(jnp.int32)

    def one_product(packed):
        child_ids, valid_row = packed
        picked = leaf_logp[child_ids]
        return jnp.sum(picked * valid_row.astype(jnp.float32)[:, None, None], axis=0)

    products = lax.map(one_product, (leaf_ids, prod_valid))

    def one_sum(carry, packed):
        child_ids, valid_row, weight_rows, flow_rows = packed
        picked = products[child_ids]
        is_valid = (valid_row > 0)[:, None, None]
        col_max = jnp.max(jnp.where(is_valid, picked, -jnp.inf), axis=(0, 1))
        scaled = jnp.where(is_valid, jnp.exp(picked - col_max), 0.0).astype(jnp.bfloat16)
        flat_rows = scaled.reshape(SE * K, TOKENS)
        totals = jnp.dot(weight_rows, flat_rows, preferred_element_type=jnp.float32)
        loglik = jnp.log(totals) + col_max
        ratios = (flow_rows / totals).astype(jnp.bfloat16)
        edge_counts = jnp.dot(ratios, flat_rows.T, preferred_element_type=jnp.float32)
        spread_back = jnp.dot(weight_rows.T, ratios, preferred_element_type=jnp.float32)
        child_flows = (flat_rows.astype(jnp.float32) * spread_back).reshape(SE, K, TOKENS)
        carry = carry.at[child_ids].add(child_flows)
        return carry, (loglik, edge_counts)

    start_flows = jnp.zeros((NBLK, K, TOKENS), jnp.float32)
    prod_flows, (sum_loglik, edge_counts) = lax.scan(one_sum, start_flows, (sum_ids, sum_valid, weights, upper_flows))
    weight_flows = weights.astype(jnp.float32) * edge_counts / TOKENS
    return sum_loglik, weight_flows, prod_flows
```

```python
import jax
import jax.numpy as jnp
from jax import lax
from jax.experimental import pallas as pl
from jax.experimental.pallas import tpu as pltpu
from jax.sharding import PartitionSpec as P

Z, X, DP = 16, 4, 8
RA = 24
RB = 32 - RA
LANE = 64
MESH = pl.DeviceIdType.MESH
F32, I32, BF16 = jnp.float32, jnp.int32, jnp.bfloat16


def place(owner):
    return ((owner & 3) << 4) + (((owner >> 2) & 3) << 2) + (owner >> 4)


def place_of(z, x):
    return x * 16 + (z % 4) * 4 + z // 4


def kernel(
    leaf_h, w_h, upper_h, leaf_asks_h, prod_asks_h, prod_child_h, prod_valid_h, sum_child_h, sum_valid_h,
    loglik_o, wflow_o, pflow_o,
    w, upper, scol, prod_asks_v, leaf_asks, prod_asks, prod_child, prod_valid, sum_child, sum_valid, insem,
    lb, ib, tbl, wt, psel, scaled, spread, acc, slot, rx, dn, r1, s2, r2, cnt, rcnt,
    ib_s, tbl_s, lsem,
    a1s, a1r, a2s, a2r, axs, axr, b1s, b1r, bxs, bxr, bzs, bzr,
    i1s, i1r, ixs, ixr, izs, izr, cs, cr_, xs, xr_, z1s, z1r, z2s, z2r,
):
    node, dp = lax.axis_index("node"), lax.axis_index("dp")
    z, x = node // X, node % X
    zc, zq = z % 4, z // 4

    def nid(zz, xx):
        return lax.rem(zz + 2 * Z, Z) * X + lax.rem(xx + 2 * X, X)

    def pos(zz, xx):
        return place_of(lax.rem(zz + 2 * Z, Z), lax.rem(xx + 2 * X, X))

    def to(zz, xx):
        return {"node": nid(zz, xx)}

    me = pos(z, x)

    def own(p, n=1):
        return pl.ds(2 * p, 2 * n)

    loads = [
        pltpu.make_async_copy(src, dst, insem.at[i])
        for i, (src, dst) in enumerate((
            (leaf_asks_h, leaf_asks), (prod_asks_h, prod_asks), (prod_child_h, prod_child),
            (prod_valid_h, prod_valid), (prod_asks_h, prod_asks_v), (leaf_h, lb.at[own(me)]),
            (sum_child_h, sum_child), (sum_valid_h, sum_valid), (sum_child_h, scol), (w_h, w), (upper_h, upper),
        ))
    ]
    for c in loads:
        c.start()
    barrier = pltpu.get_barrier_semaphore()
    for d in (1, -1, -2, 4, -4, 8):
        pl.semaphore_signal(barrier, 1, device_id=to(z + d, x), device_id_type=MESH)
    for d in (1, 2, 3):
        pl.semaphore_signal(barrier, 1, device_id=to(z, x + d), device_id_type=MESH)
    for d in range(1, DP):
        pl.semaphore_signal(barrier, 1, device_id={"dp": lax.rem(dp + d, DP)}, device_id_type=MESH)

    sends = []

    def send(src, dst, s, r, dev):
        c = pltpu.make_async_remote_copy(src, dst, s, r, device_id=dev, device_id_type=MESH)
        c.start()
        sends.append(c)

    def recv(dst, sem):
        pltpu.make_async_copy(dst, dst, sem).wait()

    lb[128] = jnp.zeros((32, 128), F32)
    for c in loads[:5]:
        c.wait()
    lane = lax.broadcasted_iota(I32, (1, 128), 1)
    row = jnp.concatenate([prod_asks_v[...], jnp.zeros((1, 64), I32)], axis=1)
    for b in range(2):
        for e in range(8):
            c = prod_child[b, e]
            where = jnp.where(prod_valid[b, e] > 0, place(c) * 2 + leaf_asks[0, c], 128)
            row = jnp.where(lane == LANE + b * 8 + e, where, row)
    ib[me] = row

    loads[5].wait()
    pl.semaphore_wait(barrier, 16)

    FAR = ((0, 1), (2, 3), (1, 2))
    NEAR = ((0, 1), (1, -1), (2, 2))
    A = lambda p: lb.at[own(p), pl.ds(0, RA), :]
    for i, j in FAR:
        send(A(me), A(me), a1s.at[i], a1r.at[i], to(z + 4 * j, x))
    for i, j in FAR:
        v = lb.at[own(me), pl.ds(RA, RB), :]
        send(v, v, b1s.at[i], b1r.at[i], to(z + 4 * j, x))
    for i, j in FAR:
        send(ib.at[me], ib.at[me], i1s.at[i], i1r.at[i], to(z + 4 * j, x))
    for i, d in NEAR:
        send(A(me), A(me), a2s.at[i, 0], a2r.at[i, 0], to(z + d, x))
    for i in range(3):
        send(A(me), A(me), axs.at[i, 0], axr.at[i], to(z, x + i + 1))

    for c in loads[6:]:
        c.wait()
    c_row = jnp.concatenate([scol[0:1, :], scol[1:2, :]], axis=1)
    ri = lax.broadcasted_iota(I32, (64, 64), 0)
    ci = lax.broadcasted_iota(I32, (64, 64), 1)
    c_col = jnp.sum(jnp.where(ri == ci, c_row, 0), axis=1, keepdims=True)
    prev = jnp.max(jnp.where((c_col == c_row) & (ci < ri), ci, -1), axis=1, keepdims=True)
    last = jnp.max(jnp.where(c_row == ri, ci, -1), axis=1, keepdims=True)
    lanes = lax.broadcasted_iota(I32, (64, 128), 1)
    both = jnp.where(lanes == 0, prev, last)
    tbl[...] = jnp.where(both < 0, 64, both)
    tcopy = pltpu.make_async_copy(tbl, tbl_s, lsem.at[0])
    tcopy.start()

    for i, j in FAR:
        p = pos(z - 4 * j, x)
        recv(A(p), a1r.at[i])
        for n, d in NEAR:
            send(A(p), A(p), a2s.at[n, i + 1], a2r.at[n, i + 1], to(z + d, x))
        for n in range(3):
            send(A(p), A(p), axs.at[n, i + 1], axr.at[n], to(z, x + n + 1))
        recv(lb.at[own(p), pl.ds(RA, RB), :], b1r.at[i])
        recv(ib.at[p], i1r.at[i])

    def cls(xx, zz):
        return xx * 16 + (lax.rem(zz + Z, Z) % 4) * 4

    def Bc(xx, zz):
        return lb.at[own(cls(xx, zz), 4), pl.ds(RA, RB), :]

    def Ic(xx, zz):
        return ib.at[pl.ds(cls(xx, zz), 4)]

    for n in range(3):
        send(Bc(x, z), Bc(x, z), bxs.at[n], bxr.at[n], to(z, x + n + 1))
        send(Ic(x, z), Ic(x, z), ixs.at[n], ixr.at[n], to(z, x + n + 1))
    for n, d in NEAR:
        send(Bc(x, z), Bc(x, z), bzs.at[n, 0], bzr.at[n], to(z + d, x))
        send(Ic(x, z), Ic(x, z), izs.at[n, 0], izr.at[n], to(z + d, x))

    def onward(k):
        for n, d in NEAR:
            p = pos(z - d - 4 * k, x)
            recv(A(p), a2r.at[n, k])
            for m in range(3):
                send(A(p), A(p), axs.at[m, 4 + n * 4 + k], axr.at[m], to(z, x + m + 1))

    onward(0)
    onward(1)
    for n in range(3):
        xx = lax.rem(x + 3 - n, X)
        recv(Bc(xx, z), bxr.at[n])
        recv(Ic(xx, z), ixr.at[n])
        for m, d in NEAR:
            send(Bc(xx, z), Bc(xx, z), bzs.at[m, n + 1], bzr.at[m], to(z + d, x))
            send(Ic(xx, z), Ic(xx, z), izs.at[m, n + 1], izr.at[m], to(z + d, x))
    onward(3)
    onward(2)

    for b in range(2):
        wt[b] = jnp.transpose(w[b].astype(F32)).astype(BF16)

    for n in range(3):
        recv(ib.at[pl.ds(0, 16)], izr.at[n])
    icopy = pltpu.make_async_copy(ib, ib_s, lsem.at[1])
    icopy.start()
    acc[64] = jnp.zeros((32, 128), F32)
    tcopy.wait()
    icopy.wait()
    for n in range(3):
        recv(lb.at[own(0, 16), pl.ds(RA, RB), :], bzr.at[n])
        recv(lb.at[own(0, 16), pl.ds(0, RA), :], axr.at[n])

    for b in range(2):

        def product(e, top, b=b):
            c = sum_child[b, e]
            base = LANE + prod_asks[0, c] * 8
            pc = place(c)
            total = None
            for j in range(8):
                v = lb[ib_s[pc, 0, base + j]]
                total = v if total is None else total + v
            psel[b * 32 + e] = total
            high = jnp.maximum(jnp.maximum(total[0:8], total[8:16]), jnp.maximum(total[16:24], total[24:32]))
            return jnp.maximum(top, jnp.where(sum_valid[b, e] > 0, high, -jnp.inf))

        top = lax.fori_loop(0, 32, product, jnp.full((8, 128), -jnp.inf, F32))
        colmax = jnp.max(top, axis=0, keepdims=True)

        def scale(e, _, b=b, colmax=colmax):
            v = jnp.where(sum_valid[b, e] > 0, jnp.exp(psel[b * 32 + e] - colmax), 0.0)
            scaled[b, pl.ds(pl.multiple_of(e * 32, 32), 32), :] = v.astype(BF16)
            return 0

        lax.fori_loop(0, 32, scale, 0)
        totals = jnp.dot(w[b], scaled[b], preferred_element_type=F32)
        loglik_o[b] = jnp.log(totals) + colmax
        ratios = (upper[b] / totals).astype(BF16)
        counts = lax.dot_general(ratios, scaled[b], (((1,), (1,)), ((), ())), preferred_element_type=F32)
        for d in range(DP):
            cnt[d, b] = counts[:, d * 128 : (d + 1) * 128]
        spread[b] = jnp.dot(wt[b], ratios, preferred_element_type=F32)

    for d in range(1, DP):
        other = lax.rem(dp + d, DP)
        send(cnt.at[other], rcnt.at[d - 1], cs.at[d - 1], cr_.at[d - 1], {"dp": other})

    def flow(e, _, b):
        rows = pl.ds(pl.multiple_of(e * 32, 32), 32)
        i = b * 32 + e
        acc[i] = scaled[b, rows, :].astype(F32) * spread[b, rows, :] + acc[tbl_s[i, 0]]
        return 0

    for b in range(2):
        lax.fori_loop(0, 32, lambda e, _, b=b: flow(e, _, b), 0)

    def fill(t, _):
        xx = lax.rem(x + t // 16, X)
        zz = (t % 4) * 4 + lax.rem(z + (t // 4) % 4, 4)
        slot[t] = acc[tbl_s[zz * X + xx, 1]]
        return 0

    ORDER = (2, 1, 3, 0)
    lax.fori_loop(0, 64, fill, 0)
    for c in ORDER:
        for n in (1, 2, 3):
            src = slot.at[pl.ds(n * 16 + c * 4, 4)]
            send(src, rx.at[n - 1, c], xs.at[n - 1, c], xr_.at[n - 1, c], to(z, x + n))

    for c in ORDER:
        for n in range(3):
            recv(rx.at[n, c], xr_.at[n, c])

        def merge(q, _, c=c):
            o = (q * 4 + lax.rem(z + c, 4)) * X + x
            v = slot[c * 4 + q]
            zero = jnp.zeros_like(v)
            a = prod_asks[0, o]
            d0, d1 = jnp.where(a == 0, v, zero), jnp.where(a == 0, zero, v)
            for n in range(3):
                a = ib_s[pos(z, x + 3 - n), 0, o]
                v = rx[n, c, q]
                d0, d1 = d0 + jnp.where(a == 0, v, zero), d1 + jnp.where(a == 0, zero, v)
            dn[c, q, 0] = d0
            dn[c, q, 1] = d1
            return 0

        lax.fori_loop(0, 4, merge, 0)
        if c:
            i = {2: 2, 1: 0, 3: 1}[c]
            send(dn.at[c], r1.at[i], z1s.at[i], z1r.at[i], to(z + NEAR[i][1], x))

    for i in (2, 0, 1):
        recv(r1.at[i], z1r.at[i])
    for j in (2, 1, 3, 0):
        q = lax.rem(zq + j, 4)
        s2[j] = (dn[0, q] + r1[0, q]) + (r1[1, q] + r1[2, q])
        if j:
            send(s2.at[j], r2.at[j - 1], z2s.at[j - 1], z2r.at[j - 1], to(z + 4 * j, x))

    for d in range(DP - 1):
        recv(rcnt.at[d], cr_.at[d])
    for b in range(2):
        total = cnt[dp, b]
        for d in range(DP - 1):
            total = total + rcnt[d, b]
        columns = pl.ds(pl.multiple_of(dp * 128, 128), 128)
        wflow_o[b] = w[b, :, columns].astype(F32) * total * (1.0 / 1024)

    for j in (1, 3, 2):
        recv(r2.at[j - 1], z2r.at[j - 1])
    pflow_o[...] = (s2[0] + r2[0]) + (r2[1] + r2[2])
    for c in sends:
        c.wait_send()


def local(leaf_logp, weights, upper_flows, leaf_asks, prod_asks, prod_child, prod_valid, sum_child, sum_valid):
    D = pltpu.SemaphoreType.DMA
    block = jax.ShapeDtypeStruct((2, 32, 128), F32)
    vmem, hbm = pl.BlockSpec(memory_space=pltpu.VMEM), pl.BlockSpec(memory_space=pltpu.HBM)
    V, S = pltpu.VMEM, pltpu.SMEM
    return pl.pallas_call(
        kernel,
        out_shape=(block, block, block),
        in_specs=[hbm] * 9,
        out_specs=(vmem,) * 3,
        scratch_shapes=[
            V((2, 32, 1024), BF16),
            V((2, 32, 128), F32),
            V((2, 32), I32),
            V((1, 64), I32),
            S((1, 64), I32), S((1, 64), I32), S((2, 8), I32), S((2, 8), I32), S((2, 32), I32), S((2, 32), I32),
            D((11,)),
            V((129, 32, 128), F32),
            V((64, 1, 128), I32),
            V((64, 128), I32),
            V((2, 1024, 32), BF16),
            V((64, 32, 128), F32),
            V((2, 1024, 128), BF16),
            V((2, 1024, 128), F32),
            V((65, 32, 128), F32),
            V((64, 32, 128), F32),
            V((3, 4, 4, 32, 128), F32),
            V((4, 4, 2, 32, 128), F32),
            V((3, 4, 2, 32, 128), F32),
            V((4, 2, 32, 128), F32),
            V((3, 2, 32, 128), F32),
            V((8, 2, 32, 128), F32),
            V((7, 2, 32, 128), F32),
            pltpu.SMEM((64, 1, 128), I32),
            pltpu.SMEM((64, 128), I32),
            D((2,)),
            D((3,)), D((3,)),
            D((3, 4)), D((3, 4)),
            D((3, 16)), D((3,)),
            D((3,)), D((3,)),
            D((3,)), D((3,)),
            D((3, 4)), D((3,)),
            D((3,)), D((3,)),
            D((3,)), D((3,)),
            D((3, 4)), D((3,)),
            D((7,)), D((7,)),
            D((3, 4)), D((3, 4)),
            D((3,)), D((3,)),
            D((3,)), D((3,)),
        ],
        compiler_params=pltpu.CompilerParams(
            collective_id=0, has_side_effects=True, vmem_limit_bytes=63 * 2**20
        ),
        name="em_pass",
    )(
        leaf_logp, weights, upper_flows, leaf_asks, prod_asks, prod_child, prod_valid, sum_child, sum_valid
    )


def solution(mesh):
    tok, own = P("node", None, "dp"), P("node", None)
    return jax.shard_map(
        local,
        mesh=mesh,
        in_specs=(tok, P("node", None, None), tok, own, own, own, own, own, own),
        out_specs=(tok, tok, tok),
        check_vma=False,
    )
```

```python
import jax
import jax.numpy as jnp
from jax import lax
from jax.experimental import pallas as pl
from jax.experimental.pallas import tpu as pltpu
from jax.sharding import PartitionSpec as P

Z, X, DP = 16, 4, 8
RA = 24
RB = 32 - RA
GROUPS = ((8, -6, 7, -7), (6, -4, 5, -5), (4, -2, 3, -3), (2, 0, 1, -1))
PLUS, MINUS = (0, 3, 4, 12, 9, 11), (1, 8, 5, 13, 7, 15)
LANE = 64
MESH = pl.DeviceIdType.MESH
F32, I32, BF16 = jnp.float32, jnp.int32, jnp.bfloat16


def place(owner):
    return ((owner & 3) << 4) + (((owner >> 2) & 3) << 2) + (owner >> 4)


def place_of(z, x):
    return x * 16 + (z % 4) * 4 + z // 4


def kernel(
    leaf_h, w_h, upper_h, leaf_asks_h, prod_asks_h, prod_child_h, prod_valid_h, sum_child_h, sum_valid_h,
    loglik_o, wflow_o, pflow_o,
    w, upper, scol, prod_asks_v, leaf_asks, prod_asks, prod_child, prod_valid, sum_child, sum_valid, insem,
    lb, ib, tbl, wt, psel, ratio, scaled, spread, acc, slot, rx, dn, near, up, usum, down, dsum, cnt, rcnt,
    ib_s, tbl_s, lsem,
    a1s, a1r, a2s, a2r, axs, axr, px, mx, fr, b1s, b1r, bxs, bxr, bzs, bzr,
    i1s, i1r, ixs, ixr, izs, izr, cs, cr_, xs, xr_, ns, nr, us, ur, ds_, dr,
):
    node, dp = lax.axis_index("node"), lax.axis_index("dp")
    z, x = node // X, node % X
    zc, zq = z % 4, z // 4

    def nid(zz, xx):
        return lax.rem(zz + 2 * Z, Z) * X + lax.rem(xx + 2 * X, X)

    def pos(zz, xx):
        return place_of(lax.rem(zz + 2 * Z, Z), lax.rem(xx + 2 * X, X))

    def to(zz, xx):
        return {"node": nid(zz, xx)}

    me = pos(z, x)

    def own(p, n=1):
        return pl.ds(2 * p, 2 * n)

    barrier = pltpu.get_barrier_semaphore()
    for d in (1, -1, 2, -2, 4, -4, 8):
        pl.semaphore_signal(barrier, 1, device_id=to(z + d, x), device_id_type=MESH)
    for d in (1, 2, 3):
        pl.semaphore_signal(barrier, 1, device_id=to(z, x + d), device_id_type=MESH)
    for d in range(1, DP):
        pl.semaphore_signal(barrier, 1, device_id={"dp": lax.rem(dp + d, DP)}, device_id_type=MESH)

    loads = [
        pltpu.make_async_copy(src, dst, insem.at[i])
        for i, (src, dst) in enumerate((
            (leaf_asks_h, leaf_asks), (prod_asks_h, prod_asks), (prod_child_h, prod_child),
            (prod_valid_h, prod_valid), (prod_asks_h, prod_asks_v), (leaf_h, lb.at[own(me)]),
            (sum_child_h, sum_child), (sum_valid_h, sum_valid), (sum_child_h, scol), (w_h, w), (upper_h, upper),
        ))
    ]
    for c in loads:
        c.start()
    sends = []

    def send(src, dst, s, r, dev):
        c = pltpu.make_async_remote_copy(src, dst, s, r, device_id=dev, device_id_type=MESH)
        c.start()
        sends.append(c)

    def recv(dst, sem):
        pltpu.make_async_copy(dst, dst, sem).wait()

    lb[128] = jnp.zeros((32, 128), F32)
    for c in loads[:5]:
        c.wait()
    lane = lax.broadcasted_iota(I32, (1, 128), 1)
    row = jnp.concatenate([prod_asks_v[...], jnp.zeros((1, 64), I32)], axis=1)
    for b in range(2):
        for e in range(8):
            c = prod_child[b, e]
            where = jnp.where(prod_valid[b, e] > 0, place(c) * 2 + leaf_asks[0, c], 128)
            row = jnp.where(lane == LANE + b * 8 + e, where, row)
    ib[me] = row

    loads[5].wait()
    pl.semaphore_wait(barrier, 17)

    FAR = ((0, 1), (2, 3), (1, 2))
    NEAR = ((0, 1), (1, -1), (2, 2))
    A = lambda p: lb.at[own(p), pl.ds(0, RA), :]
    for i, j in FAR:
        send(A(me), A(me), a1s.at[i], a1r.at[i], to(z + 4 * j, x))
    for i, j in FAR:
        v = lb.at[own(me), pl.ds(RA, RB), :]
        send(v, v, b1s.at[i], b1r.at[i], to(z + 4 * j, x))
    for i, j in FAR:
        send(ib.at[me], ib.at[me], i1s.at[i], i1r.at[i], to(z + 4 * j, x))
    for i, d in NEAR:
        send(A(me), A(me), a2s.at[i, 0], a2r.at[i, 0], to(z + d, x))

    def z_of(i):
        return z - 4 * i if i < 4 else z - NEAR[(i - 4) // 4][1] - 4 * (i % 4)

    def across(i):
        v = A(pos(z_of(i), x))
        send(v, v, axs.at[0, i], px.at[PLUS.index(i)] if i in PLUS else axr.at[0], to(z, x + 1))
        send(v, v, axs.at[2, i], mx.at[MINUS.index(i)] if i in MINUS else axr.at[2], to(z, x - 1))
        if i not in PLUS + MINUS:
            send(v, v, axs.at[1, i], axr.at[1], to(z, x + 2))

    def relay(*chunks):
        for i in chunks:
            if i in PLUS:
                v = A(pos(z_of(i), x - 1))
                recv(v, px.at[PLUS.index(i)])
                send(v, v, axs.at[1, i], fr.at[0], to(z, x + 1))
            else:
                v = A(pos(z_of(i), x + 1))
                recv(v, mx.at[MINUS.index(i)])
                send(v, v, axs.at[1, i], fr.at[1], to(z, x - 1))

    across(0)

    for c in loads[6:]:
        c.wait()
    c_row = jnp.concatenate([scol[0:1, :], scol[1:2, :]], axis=1)
    ri = lax.broadcasted_iota(I32, (64, 64), 0)
    ci = lax.broadcasted_iota(I32, (64, 64), 1)
    c_col = jnp.sum(jnp.where(ri == ci, c_row, 0), axis=1, keepdims=True)
    prev = jnp.max(jnp.where((c_col == c_row) & (ci < ri), ci, -1), axis=1, keepdims=True)
    last = jnp.max(jnp.where(c_row == ri, ci, -1), axis=1, keepdims=True)
    lanes = lax.broadcasted_iota(I32, (64, 128), 1)
    both = jnp.where(lanes == 0, prev, last)
    tbl[...] = jnp.where(both < 0, 64, both)
    tcopy = pltpu.make_async_copy(tbl, tbl_s, lsem.at[0])
    tcopy.start()

    for i, j in FAR:
        p = pos(z - 4 * j, x)
        recv(A(p), a1r.at[i])
        for n, d in NEAR:
            send(A(p), A(p), a2s.at[n, i + 1], a2r.at[n, i + 1], to(z + d, x))
        across(i + 1)
        if i == 2:
            relay(0)
        recv(lb.at[own(p), pl.ds(RA, RB), :], b1r.at[i])
        recv(ib.at[p], i1r.at[i])

    def cls(xx, zz):
        return xx * 16 + (lax.rem(zz + Z, Z) % 4) * 4

    def Bc(xx, zz):
        return lb.at[own(cls(xx, zz), 4), pl.ds(RA, RB), :]

    def Ic(xx, zz):
        return ib.at[pl.ds(cls(xx, zz), 4)]

    for n in range(3):
        send(Bc(x, z), Bc(x, z), bxs.at[n], bxr.at[n], to(z, x + n + 1))
        send(Ic(x, z), Ic(x, z), ixs.at[n], ixr.at[n], to(z, x + n + 1))
    for n, d in NEAR:
        send(Bc(x, z), Bc(x, z), bzs.at[n, 0], bzr.at[n], to(z + d, x))
        send(Ic(x, z), Ic(x, z), izs.at[n, 0], izr.at[n], to(z + d, x))

    def onward(k):
        for n, d in NEAR:
            p = pos(z - d - 4 * k, x)
            recv(A(p), a2r.at[n, k])
            across(4 + n * 4 + k)

    onward(0)
    relay(1, 3)
    onward(1)
    relay(4, 8, 12)
    onward(3)
    for n in range(3):
        xx = lax.rem(x + 3 - n, X)
        recv(Bc(xx, z), bxr.at[n])
        recv(Ic(xx, z), ixr.at[n])
        for m, d in NEAR:
            send(Bc(xx, z), Bc(xx, z), bzs.at[m, n + 1], bzr.at[m], to(z + d, x))
            send(Ic(xx, z), Ic(xx, z), izs.at[m, n + 1], izr.at[m], to(z + d, x))
    relay(5, 9, 13)
    onward(2)
    relay(7, 11, 15)

    for b in range(2):
        wt[b] = jnp.transpose(w[b].astype(F32)).astype(BF16)

    for n in range(3):
        recv(ib.at[pl.ds(0, 16)], izr.at[n])
    icopy = pltpu.make_async_copy(ib, ib_s, lsem.at[1])
    icopy.start()
    acc[64] = jnp.zeros((32, 128), F32)
    tcopy.wait()
    icopy.wait()
    for n in range(3):
        recv(lb.at[own(0, 16), pl.ds(RA, RB), :], bzr.at[n])
        recv(lb.at[own(0, (10, 4, 10)[n]), pl.ds(0, RA), :], axr.at[n])
    for n in range(2):
        recv(lb.at[own(0, 6), pl.ds(0, RA), :], fr.at[n])

    gathered = len(sends)

    for b in range(2):

        def product(e, top, b=b):
            c = sum_child[b, e]
            base = LANE + prod_asks[0, c] * 8
            pc = place(c)
            total = None
            for j in range(8):
                v = lb[ib_s[pc, 0, base + j]]
                total = v if total is None else total + v
            psel[b * 32 + e] = total
            high = jnp.maximum(jnp.maximum(total[0:8], total[8:16]), jnp.maximum(total[16:24], total[24:32]))
            return jnp.maximum(top, jnp.where(sum_valid[b, e] > 0, high, -jnp.inf))

        top = lax.fori_loop(0, 32, product, jnp.full((8, 128), -jnp.inf, F32), unroll=4)
        colmax = jnp.max(top, axis=0, keepdims=True)

        def scale(e, _, b=b, colmax=colmax):
            v = jnp.where(sum_valid[b, e] > 0, jnp.exp(psel[b * 32 + e] - colmax), 0.0)
            scaled[b, pl.ds(pl.multiple_of(e * 32, 32), 32), :] = v.astype(BF16)
            return 0

        lax.fori_loop(0, 32, scale, 0, unroll=4)
        totals = jnp.dot(w[b], scaled[b], preferred_element_type=F32)
        loglik_o[b] = jnp.log(totals) + colmax
        ratios = (upper[b] / totals).astype(BF16)
        ratio[b] = ratios
        spread[b] = jnp.dot(wt[b], ratios, preferred_element_type=F32)

    def flow(i, _):
        rows = pl.ds(pl.multiple_of(i % 32 * 32, 32), 32)
        b = i // 32
        acc[i] = scaled[b, rows, :].astype(F32) * spread[b, rows, :] + acc[tbl_s[i, 0]]
        return 0

    lax.fori_loop(0, 64, flow, 0, unroll=4)

    at_z = {d: lax.rem(z + d + Z, Z) for d in range(-7, 9)}
    for g in range(4):
        for n in range(4):
            for k in range(4):
                slot[n, g, k] = acc[tbl_s[at_z[GROUPS[g][k]] * X + lax.rem(x + n, X), 1]]
        for n in (1, 2, 3):
            send(slot.at[n, g], rx.at[n - 1, g], xs.at[n - 1, g], xr_.at[n - 1, g], to(z, x + n))

    for b in range(2):
        counts = lax.dot_general(ratio[b], scaled[b], (((1,), (1,)), ((), ())), preferred_element_type=F32)
        for d in range(DP):
            cnt[d, b] = counts[:, d * 128 : (d + 1) * 128]
    for d in range(1, DP):
        other = lax.rem(dp + d, DP)
        send(cnt.at[other], rcnt.at[d - 1], cs.at[d - 1], cr_.at[d - 1], {"dp": other})

    for c in sends[:gathered]:
        c.wait_send()

    peers_x = [pos(z, x + 3 - n) for n in range(3)]
    for g in range(4):
        for n in range(3):
            recv(rx.at[n, g], xr_.at[n, g])
        for k in range(4):
            o = at_z[GROUPS[g][k]] * X + x
            zero = jnp.zeros((32, 128), F32)
            d0, d1 = None, None
            for n in range(4):
                a = prod_asks[0, o] if n == 0 else ib_s[peers_x[n - 1], 0, o]
                v = slot[0, g, k] if n == 0 else rx[n - 1, g, k]
                m0, m1 = jnp.where(a == 0, v, zero), jnp.where(a == 0, zero, v)
                d0, d1 = (m0, m1) if n == 0 else (d0 + m0, d1 + m1)
            dn[g, k, 0] = d0
            dn[g, k, 1] = d1
            if k == 0 and g == 0:
                send(dn.at[0, 0], up.at[0], us.at[0], ur.at[0], to(z + 2, x))
            if k >= 2:
                send(dn.at[g, k], near.at[k - 2, g], ns.at[k - 2, g], nr.at[k - 2, g], to(z + (1 if k == 2 else -1), x))
        if g == 0:
            continue
        recv(near.at[1, g - 1], nr.at[1, g - 1])
        if g > 1:
            recv(down.at[g - 2], dr.at[g - 2])
        total = dn[g - 1, 1] + near[1, g - 1]
        dsum[g - 1] = total if g == 1 else total + down[g - 2]
        send(dsum.at[g - 1], down.at[g - 1], ds_.at[g - 1], dr.at[g - 1], to(z - 2, x))
        recv(near.at[0, g - 1], nr.at[0, g - 1])
        recv(up.at[g - 1], ur.at[g - 1])
        usum[g - 1] = (dn[g, 0] + near[0, g - 1]) + up[g - 1]
        send(usum.at[g - 1], up.at[g], us.at[g], ur.at[g], to(z + 2, x))

    for d in range(DP - 1):
        recv(rcnt.at[d], cr_.at[d])
    for b in range(2):
        total = cnt[dp, b]
        for d in range(DP - 1):
            total = total + rcnt[d, b]
        columns = pl.ds(pl.multiple_of(dp * 128, 128), 128)
        wflow_o[b] = w[b, :, columns].astype(F32) * total * (1.0 / 1024)

    recv(near.at[0, 3], nr.at[0, 3])
    recv(near.at[1, 3], nr.at[1, 3])
    own_flows = dn[3, 1] + (near[0, 3] + near[1, 3])
    recv(down.at[2], dr.at[2])
    own_flows = own_flows + down[2]
    recv(up.at[3], ur.at[3])
    pflow_o[...] = own_flows + up[3]
    for c in sends[gathered:]:
        c.wait_send()


def local(leaf_logp, weights, upper_flows, leaf_asks, prod_asks, prod_child, prod_valid, sum_child, sum_valid):
    D = pltpu.SemaphoreType.DMA
    block = jax.ShapeDtypeStruct((2, 32, 128), F32)
    vmem, hbm = pl.BlockSpec(memory_space=pltpu.VMEM), pl.BlockSpec(memory_space=pltpu.HBM)
    V, S = pltpu.VMEM, pltpu.SMEM
    return pl.pallas_call(
        kernel,
        out_shape=(block, block, block),
        in_specs=[hbm] * 9,
        out_specs=(vmem,) * 3,
        scratch_shapes=[
            V((2, 32, 1024), BF16),
            V((2, 32, 128), F32),
            V((2, 32), I32),
            V((1, 64), I32),
            S((1, 64), I32), S((1, 64), I32), S((2, 8), I32), S((2, 8), I32), S((2, 32), I32), S((2, 32), I32),
            D((11,)),
            V((129, 32, 128), F32),
            V((64, 1, 128), I32),
            V((64, 128), I32),
            V((2, 1024, 32), BF16),
            V((64, 32, 128), F32),
            V((2, 32, 128), BF16),
            V((2, 1024, 128), BF16),
            V((2, 1024, 128), F32),
            V((65, 32, 128), F32),
            V((4, 4, 4, 32, 128), F32),
            V((3, 4, 4, 32, 128), F32),
            V((4, 4, 2, 32, 128), F32),
            V((2, 4, 2, 32, 128), F32),
            V((4, 2, 32, 128), F32),
            V((3, 2, 32, 128), F32),
            V((3, 2, 32, 128), F32),
            V((3, 2, 32, 128), F32),
            V((8, 2, 32, 128), F32),
            V((7, 2, 32, 128), F32),
            pltpu.SMEM((64, 1, 128), I32),
            pltpu.SMEM((64, 128), I32),
            D((2,)),
            D((3,)), D((3,)),
            D((3, 4)), D((3, 4)),
            D((3, 16)), D((3,)), D((6,)), D((6,)), D((2,)),
            D((3,)), D((3,)),
            D((3,)), D((3,)),
            D((3, 4)), D((3,)),
            D((3,)), D((3,)),
            D((3,)), D((3,)),
            D((3, 4)), D((3,)),
            D((7,)), D((7,)),
            D((3, 4)), D((3, 4)),
            D((2, 4)), D((2, 4)),
            D((4,)), D((4,)),
            D((3,)), D((3,)),
        ],
        compiler_params=pltpu.CompilerParams(
            collective_id=0, has_side_effects=True, vmem_limit_bytes=63 * 2**20
        ),
        name="em_pass",
    )(
        leaf_logp, weights, upper_flows, leaf_asks, prod_asks, prod_child, prod_valid, sum_child, sum_valid
    )


def solution(mesh):
    tok, own = P("node", None, "dp"), P("node", None)
    return jax.shard_map(
        local,
        mesh=mesh,
        in_specs=(tok, P("node", None, None), tok, own, own, own, own, own, own),
        out_specs=(tok, tok, tok),
        check_vma=False,
    )
```

```python
import jax
import jax.numpy as jnp
from jax import lax
from jax.experimental import pallas as pl
from jax.experimental.pallas import tpu as pltpu
from jax.sharding import PartitionSpec as P

Z, X, DP = 16, 4, 8
RA = 24
RB = 32 - RA
GROUPS = ((8, -6, 7, -7), (6, -4, 5, -5), (4, -2, 3, -3), (2, 0, 1, -1))
PLUS, MINUS = (0, 3, 4, 12, 9, 11), (1, 8, 5, 13, 7, 15)
LANE = 64
MESH = pl.DeviceIdType.MESH
F32, I32, BF16 = jnp.float32, jnp.int32, jnp.bfloat16


def place(owner):
    return ((owner & 3) << 4) + (((owner >> 2) & 3) << 2) + (owner >> 4)


def place_of(z, x):
    return x * 16 + (z % 4) * 4 + z // 4


def kernel(
    leaf_h, w_h, upper_h, leaf_asks_h, prod_asks_h, prod_child_h, prod_valid_h, sum_child_h, sum_valid_h,
    loglik_o, wflow_o, pflow_o,
    w, upper, scol, prod_asks_v, leaf_asks, prod_asks, prod_child, prod_valid, sum_child, sum_valid, insem,
    lb, ib, tbl, wt, psel, ratio, scaled, spread, acc, slot, rx, dn, near, up, usum, down, dsum, cnt, rcnt,
    ib_s, tbl_s, lsem,
    a1s, a1r, a2s, a2r, axs, axr, px, mx, fr, b1s, b1r, bxs, bxr, bzs, bzr,
    i1s, i1r, ixs, ixr, izs, izr, cs, cr_, xs, xr_, ns, nr, us, ur, ds_, dr,
):
    node, dp = lax.axis_index("node"), lax.axis_index("dp")
    z, x = node // X, node % X
    zc, zq = z % 4, z // 4

    def nid(zz, xx):
        return lax.rem(zz + 2 * Z, Z) * X + lax.rem(xx + 2 * X, X)

    def pos(zz, xx):
        return place_of(lax.rem(zz + 2 * Z, Z), lax.rem(xx + 2 * X, X))

    def to(zz, xx):
        return {"node": nid(zz, xx)}

    me = pos(z, x)

    def own(p, n=1):
        return pl.ds(2 * p, 2 * n)

    barrier = pltpu.get_barrier_semaphore()
    for d in (1, -1, 2, -2, 4, -4, 8):
        pl.semaphore_signal(barrier, 1, device_id=to(z + d, x), device_id_type=MESH)
    for d in (1, 2, 3):
        pl.semaphore_signal(barrier, 1, device_id=to(z, x + d), device_id_type=MESH)
    for d in range(1, DP):
        pl.semaphore_signal(barrier, 1, device_id={"dp": lax.rem(dp + d, DP)}, device_id_type=MESH)

    loads = [
        pltpu.make_async_copy(src, dst, insem.at[i])
        for i, (src, dst) in enumerate((
            (leaf_asks_h, leaf_asks), (prod_asks_h, prod_asks), (prod_child_h, prod_child),
            (prod_valid_h, prod_valid), (prod_asks_h, prod_asks_v), (leaf_h, lb.at[own(me)]),
            (sum_child_h, sum_child), (sum_valid_h, sum_valid), (sum_child_h, scol), (w_h, w), (upper_h, upper),
        ))
    ]
    for c in loads:
        c.start()
    sends = []

    def send(src, dst, s, r, dev):
        c = pltpu.make_async_remote_copy(src, dst, s, r, device_id=dev, device_id_type=MESH)
        c.start()
        sends.append(c)

    def recv(dst, sem):
        pltpu.make_async_copy(dst, dst, sem).wait()

    lb[128] = jnp.zeros((32, 128), F32)
    for c in loads[:5]:
        c.wait()
    lane = lax.broadcasted_iota(I32, (1, 128), 1)
    row = jnp.concatenate([prod_asks_v[...], jnp.zeros((1, 64), I32)], axis=1)
    for b in range(2):
        for e in range(8):
            c = prod_child[b, e]
            where = jnp.where(prod_valid[b, e] > 0, place(c) * 2 + leaf_asks[0, c], 128)
            row = jnp.where(lane == LANE + b * 8 + e, where, row)
    ib[me] = row

    loads[5].wait()
    pl.semaphore_wait(barrier, 17)

    FAR = ((0, 1), (2, 3), (1, 2))
    NEAR = ((0, 1), (1, -1), (2, 2))
    A = lambda p: lb.at[own(p), pl.ds(0, RA), :]
    for i, j in FAR:
        send(ib.at[me], ib.at[me], i1s.at[i], i1r.at[i], to(z + 4 * j, x))
    for i, j in FAR:
        send(A(me), A(me), a1s.at[i], a1r.at[i], to(z + 4 * j, x))
    for i, j in FAR:
        v = lb.at[own(me), pl.ds(RA, RB), :]
        send(v, v, b1s.at[i], b1r.at[i], to(z + 4 * j, x))
    for i, d in NEAR:
        send(A(me), A(me), a2s.at[i, 0], a2r.at[i, 0], to(z + d, x))

    def z_of(i):
        return z - 4 * i if i < 4 else z - NEAR[(i - 4) // 4][1] - 4 * (i % 4)

    def across(i):
        v = A(pos(z_of(i), x))
        send(v, v, axs.at[0, i], px.at[PLUS.index(i)] if i in PLUS else axr.at[0], to(z, x + 1))
        send(v, v, axs.at[2, i], mx.at[MINUS.index(i)] if i in MINUS else axr.at[2], to(z, x - 1))
        if i not in PLUS + MINUS:
            send(v, v, axs.at[1, i], axr.at[1], to(z, x + 2))

    def relay(*chunks):
        for i in chunks:
            if i in PLUS:
                v = A(pos(z_of(i), x - 1))
                recv(v, px.at[PLUS.index(i)])
                send(v, v, axs.at[1, i], fr.at[0], to(z, x + 1))
            else:
                v = A(pos(z_of(i), x + 1))
                recv(v, mx.at[MINUS.index(i)])
                send(v, v, axs.at[1, i], fr.at[1], to(z, x - 1))

    across(0)

    for c in loads[6:]:
        c.wait()
    c_row = jnp.concatenate([scol[0:1, :], scol[1:2, :]], axis=1)
    ri = lax.broadcasted_iota(I32, (64, 64), 0)
    ci = lax.broadcasted_iota(I32, (64, 64), 1)
    c_col = jnp.sum(jnp.where(ri == ci, c_row, 0), axis=1, keepdims=True)
    prev = jnp.max(jnp.where((c_col == c_row) & (ci < ri), ci, -1), axis=1, keepdims=True)
    last = jnp.max(jnp.where(c_row == ri, ci, -1), axis=1, keepdims=True)
    lanes = lax.broadcasted_iota(I32, (64, 128), 1)
    both = jnp.where(lanes == 0, prev, last)
    tbl[...] = jnp.where(both < 0, 64, both)
    tcopy = pltpu.make_async_copy(tbl, tbl_s, lsem.at[0])
    tcopy.start()

    for b in range(2):
        wt[b] = jnp.transpose(w[b].astype(F32)).astype(BF16)

    for i, j in FAR:
        p = pos(z - 4 * j, x)
        recv(A(p), a1r.at[i])
        for n, d in NEAR:
            send(A(p), A(p), a2s.at[n, i + 1], a2r.at[n, i + 1], to(z + d, x))
        across(i + 1)
        if i == 2:
            relay(0)
        recv(lb.at[own(p), pl.ds(RA, RB), :], b1r.at[i])
        recv(ib.at[p], i1r.at[i])

    def cls(xx, zz):
        return xx * 16 + (lax.rem(zz + Z, Z) % 4) * 4

    def Bc(xx, zz):
        return lb.at[own(cls(xx, zz), 4), pl.ds(RA, RB), :]

    def Ic(xx, zz):
        return ib.at[pl.ds(cls(xx, zz), 4)]

    for n in range(3):
        send(Bc(x, z), Bc(x, z), bxs.at[n], bxr.at[n], to(z, x + n + 1))
        send(Ic(x, z), Ic(x, z), ixs.at[n], ixr.at[n], to(z, x + n + 1))
    for n, d in NEAR:
        send(Bc(x, z), Bc(x, z), bzs.at[n, 0], bzr.at[n], to(z + d, x))
        send(Ic(x, z), Ic(x, z), izs.at[n, 0], izr.at[n], to(z + d, x))

    def onward(k):
        for n, d in NEAR:
            p = pos(z - d - 4 * k, x)
            recv(A(p), a2r.at[n, k])
            across(4 + n * 4 + k)

    onward(0)
    relay(1, 3)
    onward(1)
    for n in range(3):
        xx = lax.rem(x + 3 - n, X)
        recv(Bc(xx, z), bxr.at[n])
        recv(Ic(xx, z), ixr.at[n])
        for m, d in NEAR:
            send(Bc(xx, z), Bc(xx, z), bzs.at[m, n + 1], bzr.at[m], to(z + d, x))
            send(Ic(xx, z), Ic(xx, z), izs.at[m, n + 1], izr.at[m], to(z + d, x))
    relay(4, 8, 12)
    onward(3)
    relay(5, 9, 13)
    onward(2)
    relay(7, 11, 15)

    for n in range(3):
        recv(ib.at[pl.ds(0, 16)], izr.at[n])
    icopy = pltpu.make_async_copy(ib, ib_s, lsem.at[1])
    icopy.start()
    acc[64] = jnp.zeros((32, 128), F32)
    tcopy.wait()
    icopy.wait()
    for n in range(3):
        recv(lb.at[own(0, 16), pl.ds(RA, RB), :], bzr.at[n])
        recv(lb.at[own(0, (10, 4, 10)[n]), pl.ds(0, RA), :], axr.at[n])
    for n in range(2):
        recv(lb.at[own(0, 6), pl.ds(0, RA), :], fr.at[n])

    gathered = len(sends)

    for b in range(2):

        def product(e, top, b=b):
            c = sum_child[b, e]
            base = LANE + prod_asks[0, c] * 8
            pc = place(c)
            total = None
            for j in range(8):
                v = lb[ib_s[pc, 0, base + j]]
                total = v if total is None else total + v
            psel[b * 32 + e] = total
            high = jnp.maximum(jnp.maximum(total[0:8], total[8:16]), jnp.maximum(total[16:24], total[24:32]))
            return jnp.maximum(top, jnp.where(sum_valid[b, e] > 0, high, -jnp.inf))

        top = lax.fori_loop(0, 32, product, jnp.full((8, 128), -jnp.inf, F32), unroll=4)
        colmax = jnp.max(top, axis=0, keepdims=True)

        def scale(e, _, b=b, colmax=colmax):
            v = jnp.where(sum_valid[b, e] > 0, jnp.exp(psel[b * 32 + e] - colmax), 0.0)
            scaled[b, pl.ds(pl.multiple_of(e * 32, 32), 32), :] = v.astype(BF16)
            return 0

        lax.fori_loop(0, 32, scale, 0, unroll=4)
        totals = jnp.dot(w[b], scaled[b], preferred_element_type=F32)
        loglik_o[b] = jnp.log(totals) + colmax
        ratios = (upper[b] / totals).astype(BF16)
        ratio[b] = ratios
        spread[b] = jnp.dot(wt[b], ratios, preferred_element_type=F32)

    def flow(i, _):
        rows = pl.ds(pl.multiple_of(i % 32 * 32, 32), 32)
        b = i // 32
        acc[i] = scaled[b, rows, :].astype(F32) * spread[b, rows, :] + acc[tbl_s[i, 0]]
        return 0

    lax.fori_loop(0, 64, flow, 0, unroll=4)

    at_z = {d: lax.rem(z + d + Z, Z) for d in range(-7, 9)}
    for g in range(4):
        for n in range(4):
            for k in range(4):
                slot[n, g, k] = acc[tbl_s[at_z[GROUPS[g][k]] * X + lax.rem(x + n, X), 1]]
        for n in (1, 2, 3):
            send(slot.at[n, g], rx.at[n - 1, g], xs.at[n - 1, g], xr_.at[n - 1, g], to(z, x + n))

    for b in range(2):
        counts = lax.dot_general(ratio[b], scaled[b], (((1,), (1,)), ((), ())), preferred_element_type=F32)
        for d in range(DP):
            cnt[d, b] = counts[:, d * 128 : (d + 1) * 128]
    for d in range(1, DP):
        other = lax.rem(dp + d, DP)
        send(cnt.at[other], rcnt.at[d - 1], cs.at[d - 1], cr_.at[d - 1], {"dp": other})

    for c in sends[:gathered]:
        c.wait_send()

    peers_x = [pos(z, x + 3 - n) for n in range(3)]
    for g in range(4):
        for n in range(3):
            recv(rx.at[n, g], xr_.at[n, g])
        for k in range(4):
            o = at_z[GROUPS[g][k]] * X + x
            zero = jnp.zeros((32, 128), F32)
            d0, d1 = None, None
            for n in range(4):
                a = prod_asks[0, o] if n == 0 else ib_s[peers_x[n - 1], 0, o]
                v = slot[0, g, k] if n == 0 else rx[n - 1, g, k]
                m0, m1 = jnp.where(a == 0, v, zero), jnp.where(a == 0, zero, v)
                d0, d1 = (m0, m1) if n == 0 else (d0 + m0, d1 + m1)
            dn[g, k, 0] = d0
            dn[g, k, 1] = d1
            if k == 0 and g == 0:
                send(dn.at[0, 0], up.at[0], us.at[0], ur.at[0], to(z + 2, x))
            if k >= 2:
                send(dn.at[g, k], near.at[k - 2, g], ns.at[k - 2, g], nr.at[k - 2, g], to(z + (1 if k == 2 else -1), x))
        if g == 0:
            continue
        recv(near.at[1, g - 1], nr.at[1, g - 1])
        if g > 1:
            recv(down.at[g - 2], dr.at[g - 2])
        total = dn[g - 1, 1] + near[1, g - 1]
        dsum[g - 1] = total if g == 1 else total + down[g - 2]
        send(dsum.at[g - 1], down.at[g - 1], ds_.at[g - 1], dr.at[g - 1], to(z - 2, x))
        recv(near.at[0, g - 1], nr.at[0, g - 1])
        recv(up.at[g - 1], ur.at[g - 1])
        usum[g - 1] = (dn[g, 0] + near[0, g - 1]) + up[g - 1]
        send(usum.at[g - 1], up.at[g], us.at[g], ur.at[g], to(z + 2, x))

    for d in range(DP - 1):
        recv(rcnt.at[d], cr_.at[d])
    for b in range(2):
        total = cnt[dp, b]
        for d in range(DP - 1):
            total = total + rcnt[d, b]
        columns = pl.ds(pl.multiple_of(dp * 128, 128), 128)
        wflow_o[b] = w[b, :, columns].astype(F32) * total * (1.0 / 1024)

    recv(near.at[0, 3], nr.at[0, 3])
    recv(near.at[1, 3], nr.at[1, 3])
    own_flows = dn[3, 1] + (near[0, 3] + near[1, 3])
    recv(down.at[2], dr.at[2])
    own_flows = own_flows + down[2]
    recv(up.at[3], ur.at[3])
    pflow_o[...] = own_flows + up[3]
    for c in sends[gathered:]:
        c.wait_send()


def hand_over(a, b, c, a_o, b_o, c_o):
    a_o[...] = a[...]
    b_o[...] = b[...]
    c_o[...] = c[...]


def local(leaf_logp, weights, upper_flows, leaf_asks, prod_asks, prod_child, prod_valid, sum_child, sum_valid):
    D = pltpu.SemaphoreType.DMA
    block = jax.ShapeDtypeStruct((2, 32, 128), F32)
    vmem, hbm = pl.BlockSpec(memory_space=pltpu.VMEM), pl.BlockSpec(memory_space=pltpu.HBM)
    V, S = pltpu.VMEM, pltpu.SMEM
    made = pl.pallas_call(
        kernel,
        out_shape=(block, block, block),
        in_specs=[hbm] * 9,
        out_specs=(vmem,) * 3,
        scratch_shapes=[
            V((2, 32, 1024), BF16),
            V((2, 32, 128), F32),
            V((2, 32), I32),
            V((1, 64), I32),
            S((1, 64), I32), S((1, 64), I32), S((2, 8), I32), S((2, 8), I32), S((2, 32), I32), S((2, 32), I32),
            D((11,)),
            V((129, 32, 128), F32),
            V((64, 1, 128), I32),
            V((64, 128), I32),
            V((2, 1024, 32), BF16),
            V((64, 32, 128), F32),
            V((2, 32, 128), BF16),
            V((2, 1024, 128), BF16),
            V((2, 1024, 128), F32),
            V((65, 32, 128), F32),
            V((4, 4, 4, 32, 128), F32),
            V((3, 4, 4, 32, 128), F32),
            V((4, 4, 2, 32, 128), F32),
            V((2, 4, 2, 32, 128), F32),
            V((4, 2, 32, 128), F32),
            V((3, 2, 32, 128), F32),
            V((3, 2, 32, 128), F32),
            V((3, 2, 32, 128), F32),
            V((8, 2, 32, 128), F32),
            V((7, 2, 32, 128), F32),
            pltpu.SMEM((64, 1, 128), I32),
            pltpu.SMEM((64, 128), I32),
            D((2,)),
            D((3,)), D((3,)),
            D((3, 4)), D((3, 4)),
            D((3, 16)), D((3,)), D((6,)), D((6,)), D((2,)),
            D((3,)), D((3,)),
            D((3,)), D((3,)),
            D((3, 4)), D((3,)),
            D((3,)), D((3,)),
            D((3,)), D((3,)),
            D((3, 4)), D((3,)),
            D((7,)), D((7,)),
            D((3, 4)), D((3, 4)),
            D((2, 4)), D((2, 4)),
            D((4,)), D((4,)),
            D((3,)), D((3,)),
        ],
        compiler_params=pltpu.CompilerParams(
            collective_id=0, has_side_effects=True, vmem_limit_bytes=63 * 2**20
        ),
        name="em_pass",
    )(
        leaf_logp, weights, upper_flows, leaf_asks, prod_asks, prod_child, prod_valid, sum_child, sum_valid
    )
    return pl.pallas_call(
        hand_over,
        out_shape=(block, block, block),
        in_specs=[vmem] * 3,
        out_specs=(vmem,) * 3,
        compiler_params=pltpu.CompilerParams(vmem_limit_bytes=63 * 2**20),
        name="hand_over",
    )(*made)


def solution(mesh):
    tok, own = P("node", None, "dp"), P("node", None)
    return jax.shard_map(
        local,
        mesh=mesh,
        in_specs=(tok, P("node", None, None), tok, own, own, own, own, own, own),
        out_specs=(tok, tok, tok),
        check_vma=False,
    )
```

```python
import jax
import jax.numpy as jnp
from jax import lax
from jax.experimental import pallas as pl
from jax.experimental.pallas import tpu as pltpu
from jax.sharding import PartitionSpec as P

Z, X, DP = 16, 4, 8
RA = 24
RB = 32 - RA
GROUPS = ((8, -6, 7, -7), (6, -4, 5, -5), (4, -2, 3, -3), (2, 0, 1, -1))
PLUS, MINUS = (0, 3, 4, 12, 9, 11), (1, 8, 5, 13, 7, 15)
LANE = 64
MESH = pl.DeviceIdType.MESH
F32, I32, BF16 = jnp.float32, jnp.int32, jnp.bfloat16


def place(owner):
    return ((owner & 3) << 4) + (((owner >> 2) & 3) << 2) + (owner >> 4)


def place_of(z, x):
    return x * 16 + (z % 4) * 4 + z // 4


def kernel(
    leaf_h, w_h, upper_h, leaf_asks_h, prod_asks_h, prod_child_h, prod_valid_h, sum_child_h, sum_valid_h,
    loglik_o, wflow_o, pflow_o,
    w, upper, scol, prod_asks_v, leaf_asks, prod_asks, prod_child, prod_valid, sum_child, sum_valid, insem,
    lb, ib, tbl, wt, psel, ratio, scaled, spread, acc, slot, rx, dn, near, up, usum, down, dsum, cnt, rcnt,
    ib_s, tbl_s, lsem,
    a1s, a1r, a2s, a2r, axs, axr, px, mx, fr, b1s, b1r, bxs, bxr, bzs, bzr,
    i1s, i1r, ixs, ixr, izs, izr, cs, cr_, xs, xr_, ns, nr, us, ur, ds_, dr,
):
    node, dp = lax.axis_index("node"), lax.axis_index("dp")
    z, x = node // X, node % X
    zc, zq = z % 4, z // 4

    def nid(zz, xx):
        return lax.rem(zz + 2 * Z, Z) * X + lax.rem(xx + 2 * X, X)

    def pos(zz, xx):
        return place_of(lax.rem(zz + 2 * Z, Z), lax.rem(xx + 2 * X, X))

    def to(zz, xx):
        return {"node": nid(zz, xx)}

    me = pos(z, x)

    def own(p, n=1):
        return pl.ds(2 * p, 2 * n)

    barrier = pltpu.get_barrier_semaphore()
    for d in (1, -1, 2, -2, 4, -4, 8):
        pl.semaphore_signal(barrier, 1, device_id=to(z + d, x), device_id_type=MESH)
    for d in (1, 2, 3):
        pl.semaphore_signal(barrier, 1, device_id=to(z, x + d), device_id_type=MESH)
    for d in range(1, DP):
        pl.semaphore_signal(barrier, 1, device_id={"dp": lax.rem(dp + d, DP)}, device_id_type=MESH)

    loads = [
        pltpu.make_async_copy(src, dst, insem.at[i])
        for i, (src, dst) in enumerate((
            (leaf_asks_h, leaf_asks), (prod_asks_h, prod_asks), (prod_child_h, prod_child),
            (prod_valid_h, prod_valid), (prod_asks_h, prod_asks_v), (leaf_h, lb.at[own(me)]),
            (sum_child_h, sum_child), (sum_valid_h, sum_valid), (sum_child_h, scol), (w_h, w), (upper_h, upper),
        ))
    ]
    for c in loads:
        c.start()
    sends = []

    def send(src, dst, s, r, dev):
        c = pltpu.make_async_remote_copy(src, dst, s, r, device_id=dev, device_id_type=MESH)
        c.start()
        sends.append(c)

    def recv(dst, sem):
        pltpu.make_async_copy(dst, dst, sem).wait()

    lb[128] = jnp.zeros((32, 128), F32)
    for c in loads[:5]:
        c.wait()
    lane = lax.broadcasted_iota(I32, (1, 128), 1)
    row = jnp.concatenate([prod_asks_v[...], jnp.zeros((1, 64), I32)], axis=1)
    for b in range(2):
        for e in range(8):
            c = prod_child[b, e]
            where = jnp.where(prod_valid[b, e] > 0, place(c) * 2 + leaf_asks[0, c], 128)
            row = jnp.where(lane == LANE + b * 8 + e, where, row)
    ib[me] = row

    loads[5].wait()
    pl.semaphore_wait(barrier, 17)

    FAR = ((0, 1), (2, 3), (1, 2))
    NEAR = ((0, 1), (1, -1), (2, 2))
    A = lambda p: lb.at[own(p), pl.ds(0, RA), :]
    for i, j in FAR:
        send(ib.at[me], ib.at[me], i1s.at[i], i1r.at[i], to(z + 4 * j, x))
    for i, j in FAR:
        send(A(me), A(me), a1s.at[i], a1r.at[i], to(z + 4 * j, x))
    for i, j in FAR:
        v = lb.at[own(me), pl.ds(RA, RB), :]
        send(v, v, b1s.at[i], b1r.at[i], to(z + 4 * j, x))
    for i, d in NEAR:
        send(A(me), A(me), a2s.at[i, 0], a2r.at[i, 0], to(z + d, x))

    def z_of(i):
        return z - 4 * i if i < 4 else z - NEAR[(i - 4) // 4][1] - 4 * (i % 4)

    def across(i):
        v = A(pos(z_of(i), x))
        send(v, v, axs.at[0, i], px.at[PLUS.index(i)] if i in PLUS else axr.at[0], to(z, x + 1))
        send(v, v, axs.at[2, i], mx.at[MINUS.index(i)] if i in MINUS else axr.at[2], to(z, x - 1))
        if i not in PLUS + MINUS:
            send(v, v, axs.at[1, i], axr.at[1], to(z, x + 2))

    def relay(*chunks):
        for i in chunks:
            if i in PLUS:
                v = A(pos(z_of(i), x - 1))
                recv(v, px.at[PLUS.index(i)])
                send(v, v, axs.at[1, i], fr.at[0], to(z, x + 1))
            else:
                v = A(pos(z_of(i), x + 1))
                recv(v, mx.at[MINUS.index(i)])
                send(v, v, axs.at[1, i], fr.at[1], to(z, x - 1))

    across(0)

    for c in loads[6:]:
        c.wait()
    c_row = jnp.concatenate([scol[0:1, :], scol[1:2, :]], axis=1)
    ri = lax.broadcasted_iota(I32, (64, 64), 0)
    ci = lax.broadcasted_iota(I32, (64, 64), 1)
    c_col = jnp.sum(jnp.where(ri == ci, c_row, 0), axis=1, keepdims=True)
    prev = jnp.max(jnp.where((c_col == c_row) & (ci < ri), ci, -1), axis=1, keepdims=True)
    last = jnp.max(jnp.where(c_row == ri, ci, -1), axis=1, keepdims=True)
    lanes = lax.broadcasted_iota(I32, (64, 128), 1)
    both = jnp.where(lanes == 0, prev, last)
    tbl[...] = jnp.where(both < 0, 64, both)
    tcopy = pltpu.make_async_copy(tbl, tbl_s, lsem.at[0])
    tcopy.start()

    for b in range(2):
        wt[b] = jnp.transpose(w[b].astype(F32)).astype(BF16)

    for i, j in FAR:
        p = pos(z - 4 * j, x)
        recv(A(p), a1r.at[i])
        for n, d in NEAR:
            send(A(p), A(p), a2s.at[n, i + 1], a2r.at[n, i + 1], to(z + d, x))
        across(i + 1)
        if i == 2:
            relay(0)
        recv(lb.at[own(p), pl.ds(RA, RB), :], b1r.at[i])
        recv(ib.at[p], i1r.at[i])

    def cls(xx, zz):
        return xx * 16 + (lax.rem(zz + Z, Z) % 4) * 4

    def Bc(xx, zz):
        return lb.at[own(cls(xx, zz), 4), pl.ds(RA, RB), :]

    def Ic(xx, zz):
        return ib.at[pl.ds(cls(xx, zz), 4)]

    for n in range(3):
        send(Bc(x, z), Bc(x, z), bxs.at[n], bxr.at[n], to(z, x + n + 1))
        send(Ic(x, z), Ic(x, z), ixs.at[n], ixr.at[n], to(z, x + n + 1))
    for n, d in NEAR:
        send(Bc(x, z), Bc(x, z), bzs.at[n, 0], bzr.at[n], to(z + d, x))
        send(Ic(x, z), Ic(x, z), izs.at[n, 0], izr.at[n], to(z + d, x))

    def onward(k):
        for n, d in NEAR:
            p = pos(z - d - 4 * k, x)
            recv(A(p), a2r.at[n, k])
            across(4 + n * 4 + k)

    onward(0)
    relay(1, 3)
    onward(1)
    for n in range(3):
        xx = lax.rem(x + 3 - n, X)
        recv(Bc(xx, z), bxr.at[n])
        recv(Ic(xx, z), ixr.at[n])
        for m, d in NEAR:
            send(Bc(xx, z), Bc(xx, z), bzs.at[m, n + 1], bzr.at[m], to(z + d, x))
            send(Ic(xx, z), Ic(xx, z), izs.at[m, n + 1], izr.at[m], to(z + d, x))
    relay(4, 8, 12)
    onward(3)
    relay(5, 9, 13)
    onward(2)
    relay(7, 11, 15)

    for n in range(3):
        recv(ib.at[pl.ds(0, 16)], izr.at[n])
    icopy = pltpu.make_async_copy(ib, ib_s, lsem.at[1])
    icopy.start()
    acc[64] = jnp.zeros((32, 128), F32)
    tcopy.wait()
    icopy.wait()
    for n in range(3):
        recv(lb.at[own(0, 16), pl.ds(RA, RB), :], bzr.at[n])
        recv(lb.at[own(0, (10, 4, 10)[n]), pl.ds(0, RA), :], axr.at[n])
    for n in range(2):
        recv(lb.at[own(0, 6), pl.ds(0, RA), :], fr.at[n])

    gathered = len(sends)

    for b in range(2):

        def product(e, top, b=b):
            c = sum_child[b, e]
            base = LANE + prod_asks[0, c] * 8
            pc = place(c)
            total = None
            for j in range(8):
                v = lb[ib_s[pc, 0, base + j]]
                total = v if total is None else total + v
            psel[b * 32 + e] = total
            high = jnp.maximum(jnp.maximum(total[0:8], total[8:16]), jnp.maximum(total[16:24], total[24:32]))
            return jnp.maximum(top, jnp.where(sum_valid[b, e] > 0, high, -jnp.inf))

        top = lax.fori_loop(0, 32, product, jnp.full((8, 128), -jnp.inf, F32), unroll=8)
        colmax = jnp.max(top, axis=0, keepdims=True)

        def scale(e, _, b=b, colmax=colmax):
            v = jnp.where(sum_valid[b, e] > 0, jnp.exp(psel[b * 32 + e] - colmax), 0.0)
            scaled[b, pl.ds(pl.multiple_of(e * 32, 32), 32), :] = v.astype(BF16)
            return 0

        lax.fori_loop(0, 32, scale, 0, unroll=8)
        totals = jnp.dot(w[b], scaled[b], preferred_element_type=F32)
        loglik_o[b] = jnp.log(totals) + colmax
        ratios = (upper[b] / totals).astype(BF16)
        ratio[b] = ratios
        spread[b] = jnp.dot(wt[b], ratios, preferred_element_type=F32)

    def flow(i, _):
        rows = pl.ds(pl.multiple_of(i % 32 * 32, 32), 32)
        b = i // 32
        acc[i] = scaled[b, rows, :].astype(F32) * spread[b, rows, :] + acc[tbl_s[i, 0]]
        return 0

    lax.fori_loop(0, 64, flow, 0, unroll=8)

    at_z = {d: lax.rem(z + d + Z, Z) for d in range(-7, 9)}
    for g in range(4):
        for n in range(4):
            for k in range(4):
                slot[n, g, k] = acc[tbl_s[at_z[GROUPS[g][k]] * X + lax.rem(x + n, X), 1]]
        for n in (1, 2, 3):
            send(slot.at[n, g], rx.at[n - 1, g], xs.at[n - 1, g], xr_.at[n - 1, g], to(z, x + n))

    for b in range(2):
        counts = lax.dot_general(ratio[b], scaled[b], (((1,), (1,)), ((), ())), preferred_element_type=F32)
        for d in range(DP):
            cnt[d, b] = counts[:, d * 128 : (d + 1) * 128]
    for d in range(1, DP):
        other = lax.rem(dp + d, DP)
        send(cnt.at[other], rcnt.at[d - 1], cs.at[d - 1], cr_.at[d - 1], {"dp": other})

    for c in sends[:gathered]:
        c.wait_send()

    peers_x = [pos(z, x + 3 - n) for n in range(3)]
    for g in range(4):
        for n in range(3):
            recv(rx.at[n, g], xr_.at[n, g])
        for k in range(4):
            o = at_z[GROUPS[g][k]] * X + x
            zero = jnp.zeros((32, 128), F32)
            d0, d1 = None, None
            for n in range(4):
                a = prod_asks[0, o] if n == 0 else ib_s[peers_x[n - 1], 0, o]
                v = slot[0, g, k] if n == 0 else rx[n - 1, g, k]
                m0, m1 = jnp.where(a == 0, v, zero), jnp.where(a == 0, zero, v)
                d0, d1 = (m0, m1) if n == 0 else (d0 + m0, d1 + m1)
            dn[g, k, 0] = d0
            dn[g, k, 1] = d1
            if k == 0 and g == 0:
                send(dn.at[0, 0], up.at[0], us.at[0], ur.at[0], to(z + 2, x))
            if k >= 2:
                send(dn.at[g, k], near.at[k - 2, g], ns.at[k - 2, g], nr.at[k - 2, g], to(z + (1 if k == 2 else -1), x))
        if g == 0:
            continue
        recv(near.at[1, g - 1], nr.at[1, g - 1])
        if g > 1:
            recv(down.at[g - 2], dr.at[g - 2])
        total = dn[g - 1, 1] + near[1, g - 1]
        dsum[g - 1] = total if g == 1 else total + down[g - 2]
        send(dsum.at[g - 1], down.at[g - 1], ds_.at[g - 1], dr.at[g - 1], to(z - 2, x))
        recv(near.at[0, g - 1], nr.at[0, g - 1])
        recv(up.at[g - 1], ur.at[g - 1])
        usum[g - 1] = (dn[g, 0] + near[0, g - 1]) + up[g - 1]
        send(usum.at[g - 1], up.at[g], us.at[g], ur.at[g], to(z + 2, x))

    for d in range(DP - 1):
        recv(rcnt.at[d], cr_.at[d])
    for b in range(2):
        total = cnt[dp, b]
        for d in range(DP - 1):
            total = total + rcnt[d, b]
        columns = pl.ds(pl.multiple_of(dp * 128, 128), 128)
        wflow_o[b] = w[b, :, columns].astype(F32) * total * (1.0 / 1024)

    recv(near.at[0, 3], nr.at[0, 3])
    recv(near.at[1, 3], nr.at[1, 3])
    own_flows = dn[3, 1] + (near[0, 3] + near[1, 3])
    recv(down.at[2], dr.at[2])
    own_flows = own_flows + down[2]
    recv(up.at[3], ur.at[3])
    pflow_o[...] = own_flows + up[3]
    for c in sends[gathered:]:
        c.wait_send()


def hand_over(a, b, c, a_o, b_o, c_o):
    a_o[...] = a[...]
    b_o[...] = b[...]
    c_o[...] = c[...]


def local(leaf_logp, weights, upper_flows, leaf_asks, prod_asks, prod_child, prod_valid, sum_child, sum_valid):
    D = pltpu.SemaphoreType.DMA
    block = jax.ShapeDtypeStruct((2, 32, 128), F32)
    vmem, hbm = pl.BlockSpec(memory_space=pltpu.VMEM), pl.BlockSpec(memory_space=pltpu.HBM)
    V, S = pltpu.VMEM, pltpu.SMEM
    made = pl.pallas_call(
        kernel,
        out_shape=(block, block, block),
        in_specs=[hbm] * 9,
        out_specs=(vmem,) * 3,
        scratch_shapes=[
            V((2, 32, 1024), BF16),
            V((2, 32, 128), F32),
            V((2, 32), I32),
            V((1, 64), I32),
            S((1, 64), I32), S((1, 64), I32), S((2, 8), I32), S((2, 8), I32), S((2, 32), I32), S((2, 32), I32),
            D((11,)),
            V((129, 32, 128), F32),
            V((64, 1, 128), I32),
            V((64, 128), I32),
            V((2, 1024, 32), BF16),
            V((64, 32, 128), F32),
            V((2, 32, 128), BF16),
            V((2, 1024, 128), BF16),
            V((2, 1024, 128), F32),
            V((65, 32, 128), F32),
            V((4, 4, 4, 32, 128), F32),
            V((3, 4, 4, 32, 128), F32),
            V((4, 4, 2, 32, 128), F32),
            V((2, 4, 2, 32, 128), F32),
            V((4, 2, 32, 128), F32),
            V((3, 2, 32, 128), F32),
            V((3, 2, 32, 128), F32),
            V((3, 2, 32, 128), F32),
            V((8, 2, 32, 128), F32),
            V((7, 2, 32, 128), F32),
            pltpu.SMEM((64, 1, 128), I32),
            pltpu.SMEM((64, 128), I32),
            D((2,)),
            D((3,)), D((3,)),
            D((3, 4)), D((3, 4)),
            D((3, 16)), D((3,)), D((6,)), D((6,)), D((2,)),
            D((3,)), D((3,)),
            D((3,)), D((3,)),
            D((3, 4)), D((3,)),
            D((3,)), D((3,)),
            D((3,)), D((3,)),
            D((3, 4)), D((3,)),
            D((7,)), D((7,)),
            D((3, 4)), D((3, 4)),
            D((2, 4)), D((2, 4)),
            D((4,)), D((4,)),
            D((3,)), D((3,)),
        ],
        compiler_params=pltpu.CompilerParams(
            collective_id=0, has_side_effects=True, vmem_limit_bytes=63 * 2**20
        ),
        name="em_pass",
    )(
        leaf_logp, weights, upper_flows, leaf_asks, prod_asks, prod_child, prod_valid, sum_child, sum_valid
    )
    return pl.pallas_call(
        hand_over,
        out_shape=(block, block, block),
        in_specs=[vmem] * 3,
        out_specs=(vmem,) * 3,
        compiler_params=pltpu.CompilerParams(vmem_limit_bytes=63 * 2**20),
        name="hand_over",
    )(*made)


def solution(mesh):
    tok, own = P("node", None, "dp"), P("node", None)
    return jax.shard_map(
        local,
        mesh=mesh,
        in_specs=(tok, P("node", None, None), tok, own, own, own, own, own, own),
        out_specs=(tok, tok, tok),
        check_vma=False,
    )
```

```python
import jax
import jax.numpy as jnp
from jax import lax
from jax.experimental import pallas as pl
from jax.experimental.pallas import tpu as pltpu
from jax.sharding import PartitionSpec as P

Z, X, DP = 16, 4, 8
RA = 24
RB = 32 - RA
GROUPS = ((8, -6, 7, -7), (6, -4, 5, -5), (4, -2, 3, -3), (2, 0, 1, -1))
PLUS, MINUS = (0, 3, 4, 12, 9, 11), (1, 8, 5, 13, 7, 15)
LANE = 64
MESH = pl.DeviceIdType.MESH
F32, I32, BF16 = jnp.float32, jnp.int32, jnp.bfloat16


def place(owner):
    return ((owner & 3) << 4) + (((owner >> 2) & 3) << 2) + (owner >> 4)


def place_of(z, x):
    return x * 16 + (z % 4) * 4 + z // 4


def kernel(
    leaf_h, w_h, upper_h, leaf_asks_h, prod_asks_h, prod_child_h, prod_valid_h, sum_child_h, sum_valid_h,
    loglik_o, wflow_o, pflow_o,
    w, upper, scol, prod_asks_v, leaf_asks, prod_asks, prod_child, prod_valid, sum_child, sum_valid, insem,
    lb, ib, tbl, wt, psel, ratio, scaled, spread, acc, slot, rx, dn, near, up, usum, down, dsum, cnt, rcnt,
    ib_s, tbl_s, lsem,
    a1s, a1r, a2s, a2r, axs, axr, px, mx, fr, b1s, b1r, bxs, bxr, bzs, bzr,
    i1s, i1r, ixs, ixr, izs, izr, cs, cr_, xs, xr_, ns, nr, us, ur, ds_, dr,
):
    node, dp = lax.axis_index("node"), lax.axis_index("dp")
    z, x = node // X, node % X
    zc, zq = z % 4, z // 4

    def nid(zz, xx):
        return lax.rem(zz + 2 * Z, Z) * X + lax.rem(xx + 2 * X, X)

    def pos(zz, xx):
        return place_of(lax.rem(zz + 2 * Z, Z), lax.rem(xx + 2 * X, X))

    def to(zz, xx):
        return {"node": nid(zz, xx)}

    me = pos(z, x)

    def own(p, n=1):
        return pl.ds(2 * p, 2 * n)

    barrier = pltpu.get_barrier_semaphore()
    for d in (1, -1, 2, -2, 4, -4, 8):
        pl.semaphore_signal(barrier, 1, device_id=to(z + d, x), device_id_type=MESH)
    for d in (1, 2, 3):
        pl.semaphore_signal(barrier, 1, device_id=to(z, x + d), device_id_type=MESH)
    for d in range(1, DP):
        pl.semaphore_signal(barrier, 1, device_id={"dp": lax.rem(dp + d, DP)}, device_id_type=MESH)

    loads = [
        pltpu.make_async_copy(src, dst, insem.at[i])
        for i, (src, dst) in enumerate((
            (leaf_asks_h, leaf_asks), (prod_asks_h, prod_asks), (prod_child_h, prod_child),
            (prod_valid_h, prod_valid), (prod_asks_h, prod_asks_v), (leaf_h, lb.at[own(me)]),
            (sum_child_h, sum_child), (sum_valid_h, sum_valid), (sum_child_h, scol), (w_h, w), (upper_h, upper),
        ))
    ]
    for c in loads:
        c.start()
    sends = []

    def send(src, dst, s, r, dev):
        c = pltpu.make_async_remote_copy(src, dst, s, r, device_id=dev, device_id_type=MESH)
        c.start()
        sends.append(c)

    def recv(dst, sem):
        pltpu.make_async_copy(dst, dst, sem).wait()

    lb[128] = jnp.zeros((32, 128), F32)
    for c in loads[:5]:
        c.wait()
    lane = lax.broadcasted_iota(I32, (1, 128), 1)
    row = jnp.concatenate([prod_asks_v[...], jnp.zeros((1, 64), I32)], axis=1)
    for b in range(2):
        for e in range(8):
            c = prod_child[b, e]
            where = jnp.where(prod_valid[b, e] > 0, place(c) * 2 + leaf_asks[0, c], 128)
            row = jnp.where(lane == LANE + b * 8 + e, where, row)
    ib[me] = row

    loads[5].wait()
    pl.semaphore_wait(barrier, 17)

    FAR = ((0, 1), (2, 3), (1, 2))
    NEAR = ((0, 1), (1, -1), (2, 2))
    A = lambda p: lb.at[own(p), pl.ds(0, RA), :]
    for i, j in FAR:
        send(ib.at[me], ib.at[me], i1s.at[i], i1r.at[i], to(z + 4 * j, x))
    for i, j in FAR:
        send(A(me), A(me), a1s.at[i], a1r.at[i], to(z + 4 * j, x))
    for i, j in FAR:
        v = lb.at[own(me), pl.ds(RA, RB), :]
        send(v, v, b1s.at[i], b1r.at[i], to(z + 4 * j, x))
    for i, d in NEAR:
        send(A(me), A(me), a2s.at[i, 0], a2r.at[i, 0], to(z + d, x))

    def z_of(i):
        return z - 4 * i if i < 4 else z - NEAR[(i - 4) // 4][1] - 4 * (i % 4)

    def across(i):
        v = A(pos(z_of(i), x))
        send(v, v, axs.at[0, i], px.at[PLUS.index(i)] if i in PLUS else axr.at[0], to(z, x + 1))
        send(v, v, axs.at[2, i], mx.at[MINUS.index(i)] if i in MINUS else axr.at[2], to(z, x - 1))
        if i not in PLUS + MINUS:
            send(v, v, axs.at[1, i], axr.at[1], to(z, x + 2))

    def relay(*chunks):
        for i in chunks:
            if i in PLUS:
                v = A(pos(z_of(i), x - 1))
                recv(v, px.at[PLUS.index(i)])
                send(v, v, axs.at[1, i], fr.at[0], to(z, x + 1))
            else:
                v = A(pos(z_of(i), x + 1))
                recv(v, mx.at[MINUS.index(i)])
                send(v, v, axs.at[1, i], fr.at[1], to(z, x - 1))

    across(0)

    for c in loads[6:]:
        c.wait()
    c_row = jnp.concatenate([scol[0:1, :], scol[1:2, :]], axis=1)
    ri = lax.broadcasted_iota(I32, (64, 64), 0)
    ci = lax.broadcasted_iota(I32, (64, 64), 1)
    c_col = jnp.sum(jnp.where(ri == ci, c_row, 0), axis=1, keepdims=True)
    prev = jnp.max(jnp.where((c_col == c_row) & (ci < ri), ci, -1), axis=1, keepdims=True)
    last = jnp.max(jnp.where(c_row == ri, ci, -1), axis=1, keepdims=True)
    lanes = lax.broadcasted_iota(I32, (64, 128), 1)
    both = jnp.where(lanes == 0, prev, last)
    tbl[...] = jnp.where(both < 0, 64, both)
    tcopy = pltpu.make_async_copy(tbl, tbl_s, lsem.at[0])
    tcopy.start()

    for b in range(2):
        wt[b] = jnp.transpose(w[b].astype(F32)).astype(BF16)

    for i, j in FAR:
        p = pos(z - 4 * j, x)
        recv(A(p), a1r.at[i])
        for n, d in NEAR:
            send(A(p), A(p), a2s.at[n, i + 1], a2r.at[n, i + 1], to(z + d, x))
        across(i + 1)
        if i == 2:
            relay(0)
        recv(lb.at[own(p), pl.ds(RA, RB), :], b1r.at[i])
        recv(ib.at[p], i1r.at[i])

    def cls(xx, zz):
        return xx * 16 + (lax.rem(zz + Z, Z) % 4) * 4

    def Bc(xx, zz):
        return lb.at[own(cls(xx, zz), 4), pl.ds(RA, RB), :]

    def Ic(xx, zz):
        return ib.at[pl.ds(cls(xx, zz), 4)]

    for n in range(3):
        send(Bc(x, z), Bc(x, z), bxs.at[n], bxr.at[n], to(z, x + n + 1))
        send(Ic(x, z), Ic(x, z), ixs.at[n], ixr.at[n], to(z, x + n + 1))
    for n, d in NEAR:
        send(Bc(x, z), Bc(x, z), bzs.at[n, 0], bzr.at[n], to(z + d, x))
        send(Ic(x, z), Ic(x, z), izs.at[n, 0], izr.at[n], to(z + d, x))

    def onward(k):
        for n, d in NEAR:
            p = pos(z - d - 4 * k, x)
            recv(A(p), a2r.at[n, k])
            across(4 + n * 4 + k)

    onward(0)
    relay(1, 3)
    onward(1)
    for n in range(3):
        xx = lax.rem(x + 3 - n, X)
        recv(Bc(xx, z), bxr.at[n])
        recv(Ic(xx, z), ixr.at[n])
        for m, d in NEAR:
            send(Bc(xx, z), Bc(xx, z), bzs.at[m, n + 1], bzr.at[m], to(z + d, x))
            send(Ic(xx, z), Ic(xx, z), izs.at[m, n + 1], izr.at[m], to(z + d, x))
    relay(4, 8, 12)
    onward(3)
    relay(5, 9, 13)
    onward(2)
    relay(7, 11, 15)

    for n in range(3):
        recv(ib.at[pl.ds(0, 16)], izr.at[n])
    icopy = pltpu.make_async_copy(ib, ib_s, lsem.at[1])
    icopy.start()
    acc[64] = jnp.zeros((32, 128), F32)
    tcopy.wait()
    icopy.wait()
    for n in range(3):
        recv(lb.at[own(0, 16), pl.ds(RA, RB), :], bzr.at[n])
        recv(lb.at[own(0, (10, 4, 10)[n]), pl.ds(0, RA), :], axr.at[n])
    for n in range(2):
        recv(lb.at[own(0, 6), pl.ds(0, RA), :], fr.at[n])

    gathered = len(sends)

    for b in range(2):

        def product(e, top, b=b):
            c = sum_child[b, e]
            base = LANE + prod_asks[0, c] * 8
            pc = place(c)
            total = None
            for j in range(8):
                v = lb[ib_s[pc, 0, base + j]]
                total = v if total is None else total + v
            psel[b * 32 + e] = total
            high = jnp.maximum(jnp.maximum(total[0:8], total[8:16]), jnp.maximum(total[16:24], total[24:32]))
            return jnp.maximum(top, jnp.where(sum_valid[b, e] > 0, high, -jnp.inf))

        top = lax.fori_loop(0, 32, product, jnp.full((8, 128), -jnp.inf, F32), unroll=8)
        colmax = jnp.max(top, axis=0, keepdims=True)

        def scale(e, _, b=b, colmax=colmax):
            v = jnp.where(sum_valid[b, e] > 0, jnp.exp(psel[b * 32 + e] - colmax), 0.0)
            scaled[b, pl.ds(pl.multiple_of(e * 32, 32), 32), :] = v.astype(BF16)
            return 0

        lax.fori_loop(0, 32, scale, 0, unroll=8)
        totals = jnp.dot(w[b], scaled[b], preferred_element_type=F32)
        loglik_o[b] = jnp.log(totals) + colmax
        ratios = (upper[b] / totals).astype(BF16)
        ratio[b] = ratios
        spread[b] = jnp.dot(wt[b], ratios, preferred_element_type=F32)

    def flow(i, _):
        rows = pl.ds(pl.multiple_of(i % 32 * 32, 32), 32)
        b = i // 32
        acc[i] = scaled[b, rows, :].astype(F32) * spread[b, rows, :] + acc[tbl_s[i, 0]]
        return 0

    lax.fori_loop(0, 64, flow, 0, unroll=8)

    at_z = {d: lax.rem(z + d + Z, Z) for d in range(-7, 9)}
    for g in range(4):
        for n in range(4):
            for k in range(4):
                slot[n, g, k] = acc[tbl_s[at_z[GROUPS[g][k]] * X + lax.rem(x + n, X), 1]]
        for n in (1, 2, 3):
            send(slot.at[n, g], rx.at[n - 1, g], xs.at[n - 1, g], xr_.at[n - 1, g], to(z, x + n))

    def count():
        for b in range(2):
            counts = lax.dot_general(ratio[b], scaled[b], (((1,), (1,)), ((), ())), preferred_element_type=F32)
            for d in range(DP):
                cnt[d, b] = counts[:, d * 128 : (d + 1) * 128]
        for d in range(1, DP):
            other = lax.rem(dp + d, DP)
            send(cnt.at[other], rcnt.at[d - 1], cs.at[d - 1], cr_.at[d - 1], {"dp": other})

    peers_x = [pos(z, x + 3 - n) for n in range(3)]
    for g in range(4):
        for n in range(3):
            recv(rx.at[n, g], xr_.at[n, g])
        for k in range(4):
            o = at_z[GROUPS[g][k]] * X + x
            zero = jnp.zeros((32, 128), F32)
            d0, d1 = None, None
            for n in range(4):
                a = prod_asks[0, o] if n == 0 else ib_s[peers_x[n - 1], 0, o]
                v = slot[0, g, k] if n == 0 else rx[n - 1, g, k]
                m0, m1 = jnp.where(a == 0, v, zero), jnp.where(a == 0, zero, v)
                d0, d1 = (m0, m1) if n == 0 else (d0 + m0, d1 + m1)
            dn[g, k, 0] = d0
            dn[g, k, 1] = d1
            if k == 0 and g == 0:
                send(dn.at[0, 0], up.at[0], us.at[0], ur.at[0], to(z + 2, x))
            if k >= 2:
                send(dn.at[g, k], near.at[k - 2, g], ns.at[k - 2, g], nr.at[k - 2, g], to(z + (1 if k == 2 else -1), x))
        if g == 0:
            count()
            continue
        for c in sends[gathered * (g - 1) // 3 : gathered * g // 3]:
            c.wait_send()
        recv(near.at[1, g - 1], nr.at[1, g - 1])
        if g > 1:
            recv(down.at[g - 2], dr.at[g - 2])
        total = dn[g - 1, 1] + near[1, g - 1]
        dsum[g - 1] = total if g == 1 else total + down[g - 2]
        send(dsum.at[g - 1], down.at[g - 1], ds_.at[g - 1], dr.at[g - 1], to(z - 2, x))
        recv(near.at[0, g - 1], nr.at[0, g - 1])
        recv(up.at[g - 1], ur.at[g - 1])
        usum[g - 1] = (dn[g, 0] + near[0, g - 1]) + up[g - 1]
        send(usum.at[g - 1], up.at[g], us.at[g], ur.at[g], to(z + 2, x))

    for d in range(DP - 1):
        recv(rcnt.at[d], cr_.at[d])
    for b in range(2):
        total = cnt[dp, b]
        for d in range(DP - 1):
            total = total + rcnt[d, b]
        columns = pl.ds(pl.multiple_of(dp * 128, 128), 128)
        wflow_o[b] = w[b, :, columns].astype(F32) * total * (1.0 / 1024)

    late = len(sends) - 8
    for c in sends[gathered:late]:
        c.wait_send()
    recv(near.at[0, 3], nr.at[0, 3])
    recv(near.at[1, 3], nr.at[1, 3])
    own_flows = dn[3, 1] + (near[0, 3] + near[1, 3])
    recv(down.at[2], dr.at[2])
    own_flows = own_flows + down[2]
    recv(up.at[3], ur.at[3])
    pflow_o[...] = own_flows + up[3]
    for c in sends[late:]:
        c.wait_send()


def hand_over(a, b, c, a_o, b_o, c_o):
    a_o[...] = a[...]
    b_o[...] = b[...]
    c_o[...] = c[...]


def local(leaf_logp, weights, upper_flows, leaf_asks, prod_asks, prod_child, prod_valid, sum_child, sum_valid):
    D = pltpu.SemaphoreType.DMA
    block = jax.ShapeDtypeStruct((2, 32, 128), F32)
    vmem, hbm = pl.BlockSpec(memory_space=pltpu.VMEM), pl.BlockSpec(memory_space=pltpu.HBM)
    V, S = pltpu.VMEM, pltpu.SMEM
    made = pl.pallas_call(
        kernel,
        out_shape=(block, block, block),
        in_specs=[hbm] * 9,
        out_specs=(vmem,) * 3,
        scratch_shapes=[
            V((2, 32, 1024), BF16),
            V((2, 32, 128), F32),
            V((2, 32), I32),
            V((1, 64), I32),
            S((1, 64), I32), S((1, 64), I32), S((2, 8), I32), S((2, 8), I32), S((2, 32), I32), S((2, 32), I32),
            D((11,)),
            V((129, 32, 128), F32),
            V((64, 1, 128), I32),
            V((64, 128), I32),
            V((2, 1024, 32), BF16),
            V((64, 32, 128), F32),
            V((2, 32, 128), BF16),
            V((2, 1024, 128), BF16),
            V((2, 1024, 128), F32),
            V((65, 32, 128), F32),
            V((4, 4, 4, 32, 128), F32),
            V((3, 4, 4, 32, 128), F32),
            V((4, 4, 2, 32, 128), F32),
            V((2, 4, 2, 32, 128), F32),
            V((4, 2, 32, 128), F32),
            V((3, 2, 32, 128), F32),
            V((3, 2, 32, 128), F32),
            V((3, 2, 32, 128), F32),
            V((8, 2, 32, 128), F32),
            V((7, 2, 32, 128), F32),
            pltpu.SMEM((64, 1, 128), I32),
            pltpu.SMEM((64, 128), I32),
            D((2,)),
            D((3,)), D((3,)),
            D((3, 4)), D((3, 4)),
            D((3, 16)), D((3,)), D((6,)), D((6,)), D((2,)),
            D((3,)), D((3,)),
            D((3,)), D((3,)),
            D((3, 4)), D((3,)),
            D((3,)), D((3,)),
            D((3,)), D((3,)),
            D((3, 4)), D((3,)),
            D((7,)), D((7,)),
            D((3, 4)), D((3, 4)),
            D((2, 4)), D((2, 4)),
            D((4,)), D((4,)),
            D((3,)), D((3,)),
        ],
        compiler_params=pltpu.CompilerParams(
            collective_id=0, has_side_effects=True, vmem_limit_bytes=63 * 2**20
        ),
        name="em_pass",
    )(
        leaf_logp, weights, upper_flows, leaf_asks, prod_asks, prod_child, prod_valid, sum_child, sum_valid
    )
    return pl.pallas_call(
        hand_over,
        out_shape=(block, block, block),
        in_specs=[vmem] * 3,
        out_specs=(vmem,) * 3,
        compiler_params=pltpu.CompilerParams(vmem_limit_bytes=63 * 2**20),
        name="hand_over",
    )(*made)


def solution(mesh):
    tok, own = P("node", None, "dp"), P("node", None)
    return jax.shard_map(
        local,
        mesh=mesh,
        in_specs=(tok, P("node", None, None), tok, own, own, own, own, own, own),
        out_specs=(tok, tok, tok),
        check_vma=False,
    )
```
